512 devices in a mesh: morton: 64 (over z, y), slab: 8 (over x, core).
Axes of the slice: x: 4, y: 8, z: 8, core: 2. Of those that a mesh axis runs over, the one named last changes fastest.
Arguments:
- sources: bfloat16 [1024, 32, 256], P('morton', None, 'slab'), may hold values from -6 to 6
- basis_in: bfloat16 [1024, 64, 256], P('morton', None, 'slab'), may hold values from -0.375 to 0.375
- basis_out: bfloat16 [1024, 64, 256], P('morton', None, 'slab'), may hold values from -0.75 to 0.75
- transfer: float32 [1920, 64, 64], P('morton'), may hold values from -0.5 to 0.5
- coupling: float32 [1984, 16, 64, 64], P('morton', 'slab'), may hold values from -0.1875 to 0.1875
- coupling_list: int32 [1984, 16], P('morton', 'slab'), may hold values from 0 to 1983, as said below
- near_block: bfloat16 [12288, 256, 256], P('morton', 'slab'), may hold values from -0.15625 to 0.15625
- near_scale: float32 [12288], P('morton'), may hold values from 0.25 to 4
- near_target: int32 [12288], P('morton'), may hold values from 0 to 1023, as said below
- near_source: int32 [12288], P('morton'), may hold values from 0 to 1023, as said below
- near_count: int32 [64], P('morton'), may hold values from 48 to 192
Outputs:
- product: float32 [1024, 32, 256], P('morton', None, 'slab')
The draws below stay inside these ranges and needn't reach their ends.
Inputs may be any that keep to these rules, and one draw needn't show every extreme that they name: `coupling_list`: an entry of the list of a cluster below the top names a different cluster of the same level owned by the same index of morton or by either Morton neighbour; an entry of a top cluster's list names the top cluster of another index of morton. `near_target`: the slots of index m of morton name leaves of index m; the first 16 slots of every index name its leaves in order. `near_source`: the slots of index m of morton name leaves owned by m, m - 1 or m + 1; the first 16 slots of every index name the same leaf as near_target.
All inputs are finite; a program needn't handle non-finite values.
Results may differ from the reference program's by a relative error of at most 0.0021.
Values may be sent and summed in bfloat16 or wider, within the bound.
No kernel may reach another device: no remote copies, remote signals or barrier semaphores. Data moves between devices by JAX's collectives and lax.ppermute only.
A program may use at most 64 MiB of HBM per device.

```python
import math
import jax
import jax.numpy as jnp
import numpy as np
from jax import lax

LEAF = 256
K = 64
NRHS = 32
NCOUP = 16
LEAF_DEV = 16
NEAR_DEV = 192
CL_DEV = 31
NLEAF = 1024
NCL = 1984
NEARS = 12288
N_MORTON = 64


def draw_coupling_list(key, part):
    key = jax.random.fold_in(key, 11)
    morton_count = NLEAF // LEAF_DEV
    clusters = 2 * LEAF_DEV - 1
    offset_table = []
    count_table = []
    local_table = []
    offset = 0
    for height in range(LEAF_DEV.bit_length()):
        cluster_count = LEAF_DEV >> height
        for local in range(cluster_count):
            offset_table.append(offset)
            count_table.append(cluster_count)
            local_table.append(local)
        offset = offset + cluster_count
    level_offset = jnp.asarray(np.array(offset_table, dtype=np.int32))
    level_count = jnp.asarray(np.array(count_table, dtype=np.int32))
    level_local = jnp.asarray(np.array(local_table, dtype=np.int32))
    global_ids = jnp.arange(morton_count * clusters, dtype=jnp.int32)
    owner = global_ids // clusters
    within = global_ids % clusters
    first_key, second_key, third_key = jax.random.split(key, 3)
    shifts = jax.random.randint(first_key, (morton_count * clusters, NCOUP), -1, 2, dtype=jnp.int32)
    source_owner = jnp.clip(owner[:, None] + shifts, 0, morton_count - 1)
    row_count = level_count[within][:, None]
    row_local = level_local[within][:, None]
    chosen = jax.random.randint(second_key, (morton_count * clusters, NCOUP), 0, row_count, dtype=jnp.int32)
    clash = (source_owner == owner[:, None]) & (chosen == row_local)
    chosen = jnp.where(clash, (chosen + 1) % row_count, chosen)
    lower_ids = source_owner * clusters + level_offset[within][:, None] + chosen
    top_owner = jax.random.randint(third_key, (morton_count * clusters, NCOUP), 0, morton_count - 1, dtype=jnp.int32)
    top_owner = jnp.where(top_owner >= owner[:, None], top_owner + 1, top_owner)
    top_ids = top_owner * clusters + clusters - 1
    listed = jnp.where((within == clusters - 1)[:, None], top_ids, lower_ids)
    listed = listed.at[clusters - 1, 0].set((morton_count - 1) * clusters + clusters - 1)
    listed = listed.at[clusters, 0].set(0)
    return listed.astype(jnp.int32)


def draw_near_count(key, part):
    key = jax.random.fold_in(key, 12)
    morton_count = NLEAF // LEAF_DEV
    first_key, second_key, third_key = jax.random.split(key, 3)
    counts = jax.random.randint(first_key, (morton_count,), NEAR_DEV // 4, 3 * NEAR_DEV // 4 + 1, dtype=jnp.int32)
    heavy = jax.random.randint(second_key, (), 0, morton_count, dtype=jnp.int32)
    light = (heavy + 1 + jax.random.randint(third_key, (), 0, morton_count - 1, dtype=jnp.int32)) % morton_count
    counts = counts.at[heavy].set(NEAR_DEV)
    counts = counts.at[light].set(NEAR_DEV // 4)
    return counts.astype(jnp.int32)


def draw_near_target(key, part):
    key = jax.random.fold_in(key, 13)
    slot_ids = jnp.arange(NEARS, dtype=jnp.int32)
    owner = slot_ids // NEAR_DEV
    within = slot_ids % NEAR_DEV
    first_key, second_key = jax.random.split(key)
    first_pick = jax.random.randint(first_key, (NEARS,), 0, LEAF_DEV, dtype=jnp.int32)
    second_pick = jax.random.randint(second_key, (NEARS,), 0, LEAF_DEV, dtype=jnp.int32)
    local = jnp.where(within < LEAF_DEV, within, jnp.minimum(first_pick, second_pick))
    return (owner * LEAF_DEV + local).astype(jnp.int32)


def draw_near_source(key, part):
    key = jax.random.fold_in(key, 14)
    morton_count = NLEAF // LEAF_DEV
    slot_ids = jnp.arange(NEARS, dtype=jnp.int32)
    owner = slot_ids // NEAR_DEV
    within = slot_ids % NEAR_DEV
    first_key, second_key = jax.random.split(key)
    shifts = jax.random.randint(first_key, (NEARS,), -1, 2, dtype=jnp.int32)
    source_owner = jnp.clip(owner + shifts, 0, morton_count - 1)
    local = jax.random.randint(second_key, (NEARS,), 0, LEAF_DEV, dtype=jnp.int32)
    picked = jnp.where(within < LEAF_DEV, owner * LEAF_DEV + within, source_owner * LEAF_DEV + local)
    return picked.astype(jnp.int32)


def block_scale(rng, extent, shards, smallest, top_value):
    factor_of, own = 1.0, jax.random.fold_in(rng, 6)
    for position, blocks in shards:
        heights = jnp.exp(jax.random.uniform(jax.random.fold_in(own, position), (blocks,), jnp.float32, smallest / len(shards), top_value / len(shards)))
        factor_of = factor_of * jnp.repeat(heights, extent[position] // blocks).reshape([-1 if axis == position else 1 for axis in range(len(extent))])
    return factor_of


def gaussian(stream_key, dims, scale, limit, pieces=(), held_as=jnp.bfloat16):
    result = jax.random.normal(stream_key, dims, jnp.float32) * scale
    if len(pieces) > 0:
        result = block_scale(stream_key, dims, pieces, -0.22, 0.18) * result
    return jnp.clip(result, min=-limit, max=limit).astype(held_as)


def setup_inputs(seed: int = 0) -> dict:
    seeds = jax.random.split(jax.random.key(seed), 12)
    sources = gaussian(seeds[0], (NLEAF, NRHS, LEAF), 1.0, 6.0, ((0, 64), (2, 8)))
    basis_in = gaussian(seeds[1], (NLEAF, K, LEAF), LEAF ** -0.5, 0.375, ((0, 64), (2, 8)))
    basis_out = gaussian(seeds[2], (NLEAF, K, LEAF), K ** -0.5, 0.75, ((0, 64), (2, 8)))
    transfer = gaussian(seeds[3], ((CL_DEV - 1) * N_MORTON, K, K), (2 * K) ** -0.5, 0.5, ((0, 64),), jnp.float32)
    coupling = gaussian(seeds[4], (NCL, NCOUP, K, K), (K * NCOUP) ** -0.5, 0.1875, ((0, 64), (1, 8)), jnp.float32)
    coupling_list = draw_coupling_list(jax.random.fold_in(seeds[11], 71), 0)
    near_block = gaussian(seeds[6], (NEARS, LEAF, LEAF), (LEAF * 6) ** -0.5, 0.15625, ((0, 64), (1, 8)))
    near_scale = jnp.clip(jnp.exp(math.log(4.0) - 2.7725887 * jax.random.uniform(seeds[7], (NEARS,), jnp.float32) ** block_scale(seeds[7], (NEARS,), ((0, 64),), -0.2, 0.2)), 0.25, 4.0)
    near_target = draw_near_target(jax.random.fold_in(seeds[11], 71), 0)
    near_source = draw_near_source(jax.random.fold_in(seeds[11], 71), 0)
    near_count = draw_near_count(jax.random.fold_in(seeds[11], 71), 0)
    return {"sources": sources, "basis_in": basis_in, "basis_out": basis_out, "transfer": transfer, "coupling": coupling, "coupling_list": coupling_list, "near_block": near_block, "near_scale": near_scale, "near_target": near_target, "near_source": near_source, "near_count": near_count}


def level_sizes(leaves):
    return [leaves >> height for height in range(leaves.bit_length())]


def upward(leaf_skeleton, transfer):
    gathered_levels = [leaf_skeleton]
    current = leaf_skeleton
    offset = 0
    for cluster_count in level_sizes(leaf_skeleton.shape[0])[:-1]:
        matrices = transfer[offset:offset + cluster_count]
        carried = jnp.einsum('cij,cjr->cir', matrices, current, precision=lax.Precision.HIGHEST)
        current = carried.reshape(cluster_count // 2, 2, carried.shape[1], carried.shape[2]).sum(axis=1)
        gathered_levels.append(current)
        offset = offset + cluster_count
    return jnp.concatenate(gathered_levels, axis=0)


def downward(targets, transfer, leaves):
    counts = level_sizes(leaves)
    offsets = [sum(counts[:height]) for height in range(len(counts))]
    parent = targets[offsets[-1]:offsets[-1] + 1]
    for height in reversed(range(len(counts) - 1)):
        cluster_count = counts[height]
        offset = offsets[height]
        matrices = transfer[offset:offset + cluster_count]
        spread = jnp.repeat(parent, 2, axis=0)
        parent = targets[offset:offset + cluster_count] + jnp.einsum('cji,cjr->cir', matrices, spread, precision=lax.Precision.HIGHEST)
    return parent


def reference(sources, basis_in, basis_out, transfer, coupling, coupling_list, near_block, near_scale, near_target, near_source, near_count):
    morton_count = NLEAF // LEAF_DEV
    clusters = 2 * LEAF_DEV - 1
    leaf_skeleton = jnp.einsum('lkp,lrp->lkr', basis_in.astype(jnp.float32), sources.astype(jnp.float32), precision=lax.Precision.HIGHEST)
    skeleton = jax.vmap(upward)(leaf_skeleton.reshape(morton_count, LEAF_DEV, K, NRHS), transfer.reshape(morton_count, clusters - 1, K, K))
    skeleton = skeleton.reshape(morton_count * clusters, K, NRHS)
    picked = skeleton[coupling_list]
    target_skeleton = jnp.einsum('gekj,gejr->gkr', coupling, picked, precision=lax.Precision.HIGHEST)
    local_field = jax.vmap(lambda targets, matrices: downward(targets, matrices, LEAF_DEV))(target_skeleton.reshape(morton_count, clusters, K, NRHS), transfer.reshape(morton_count, clusters - 1, K, K))
    leaf_field = lax.optimization_barrier(local_field.reshape(NLEAF, K, NRHS).astype(jnp.bfloat16)).astype(jnp.float32)
    far_field = jnp.einsum('lkr,lkp->lrp', leaf_field, basis_out.astype(jnp.float32), precision=lax.Precision.HIGHEST)

    def one_device(items):
        blocks, source_ids, target_ids, scales, live_count, owner = items
        gathered = sources[source_ids].astype(jnp.float32)
        products = jnp.einsum('npq,nrq->nrp', blocks.astype(jnp.float32), gathered, precision=lax.Precision.HIGHEST)
        slot_ids = jnp.arange(NEAR_DEV, dtype=jnp.int32)
        weights = jnp.where(slot_ids < live_count, scales, jnp.zeros_like(scales))
        own_leaves = owner * LEAF_DEV + jnp.arange(LEAF_DEV, dtype=jnp.int32)
        selector = (target_ids[None, :] == own_leaves[:, None]).astype(jnp.float32) * weights[None, :]
        return jnp.einsum('ln,nrp->lrp', selector, products, precision=lax.Precision.HIGHEST)

    near_field = lax.map(one_device, (
        near_block.reshape(morton_count, NEAR_DEV, LEAF, LEAF),
        near_source.reshape(morton_count, NEAR_DEV),
        near_target.reshape(morton_count, NEAR_DEV),
        near_scale.reshape(morton_count, NEAR_DEV),
        near_count,
        jnp.arange(morton_count, dtype=jnp.int32)))
    near_field = near_field.reshape(NLEAF, NRHS, LEAF)
    return far_field + near_field
```

```python
import jax
import jax.numpy as jnp
from jax import lax
from jax.experimental import pallas as pl
from jax.experimental.pallas import tpu as pltpu
from jax.sharding import Mesh, PartitionSpec as P

LEAVES = 16
CLUSTERS = 31
RANK = 64
RHS = 32
POINTS = 256
SLABS = 8
PART = POINTS // SLABS
PAIRS = 15
SRC_ROWS = LEAVES * RHS * PART // 128
BASIS_ROWS = LEAVES * PART * RANK // 128
TOP_ROW = SRC_ROWS + BASIS_ROWS
OWNER_ROW = TOP_ROW + RANK
PACKED = OWNER_ROW + 16
TILE_SLOTS = 8
NEAR_CHUNKS = 4
bf16 = jnp.bfloat16
f32 = jnp.float32
MIB = 1024 * 1024
pin = pltpu.with_memory_space_constraint
HBM = pltpu.HBM
NT = (((1,), (1,)), ((), ()))
NN = (((1,), (0,)), ((), ()))


def dot(a, b, dims):
    return lax.dot_general(a, b, dims, preferred_element_type=f32)


def split(x):
    high = x.astype(bf16)
    return high, (x - high.astype(f32)).astype(bf16)


def dot3(a, b, dims):
    a_high, a_low = a
    b_high, b_low = b
    rows = a_high.shape[0]
    both = dot(jnp.concatenate([a_high, a_low], axis=0), b_high, dims)
    return both[:rows] + both[rows:] + dot(a_high, b_low, dims)


def pair_matrices(transfer_ref, i):
    return jnp.concatenate([transfer_ref[2 * i], transfer_ref[2 * i + 1]], axis=1)


def climb(pairs, transfer_ref, keep):
    first = 0
    count = LEAVES // 2
    while True:
        parents = []
        for i in range(first, first + count):
            parts = split(pairs[i])
            keep(i, parts)
            parents.append(dot3(parts, split(pair_matrices(transfer_ref, i)), NT))
        if count == 1:
            return parents[0]
        first = first + count
        count = count // 2
        for i in range(count):
            pairs.append(jnp.concatenate([parents[2 * i], parents[2 * i + 1]], axis=1))


def descend(level, transfer_ref, own):
    first = PAIRS - 1
    while first > 0:
        parents = []
        for pair in level:
            parents.append(pair[:, :RANK])
            parents.append(pair[:, RANK:])
        first = first - len(parents)
        level = []
        for i, parent in enumerate(parents):
            passed = dot3(split(parent), split(pair_matrices(transfer_ref, first + i)), NN)
            level.append(passed if own is None else own(first + i) + passed)
    return level


def leaf_pair(sources, basis):
    product = dot(jnp.concatenate(sources, axis=0), basis, NN)
    left = lax.broadcasted_iota(jnp.int32, (RHS, 128), 1) < RANK
    return jnp.where(left, product[:RHS], product[RHS:])


def fetch(pairs, sems):
    copies = [
        pltpu.make_async_copy(src, dst, sems.at[k]) for k, (src, dst) in enumerate(pairs)
    ]
    for copy in copies:
        copy.start()
    return copies


def pack_kernel(
    list_hbm,
    sources_hbm,
    basis_hbm,
    coupling_hbm,
    out_ref,
    sources_ref,
    basis_ref,
    coupling_ref,
    list_ref,
    in_sem,
):
    copies = fetch(
        (
            (sources_hbm, sources_ref),
            (basis_hbm, basis_ref),
            (coupling_hbm.at[CLUSTERS - 1], coupling_ref),
            (list_hbm, list_ref),
        ),
        in_sem,
    )
    for copy in copies:
        copy.wait()
    owners = [
        lax.shift_right_logical(list_ref[e, CLUSTERS - 1] * 2115, 16) for e in range(2)
    ]
    lane = lax.broadcasted_iota(jnp.int32, (16, 128), 1)
    out_ref[OWNER_ROW : OWNER_ROW + 16, :] = (
        jnp.where(lane == 0, owners[0], owners[1]).astype(f32).astype(bf16)
    )
    for g in range(LEAVES // 4):
        out_ref[g * RHS : (g + 1) * RHS, :] = jnp.concatenate(
            [sources_ref[4 * g + i] for i in range(4)], axis=1
        )
    for i in range(LEAVES // 2):
        start = SRC_ROWS + i * PART
        out_ref[start : start + PART, :] = jnp.concatenate(
            [basis_ref[2 * i], basis_ref[2 * i + 1]], axis=1
        )
    out_ref[TOP_ROW : TOP_ROW + RANK, :] = jnp.concatenate(
        [coupling_ref[0], coupling_ref[1]], axis=1
    ).astype(bf16)


def up_kernel(
    packed_hbm,
    transfer_ref,
    mine_hbm,
    top_hbm,
    matrix_hbm,
    owner_ref,
    sources_ref,
    basis_ref,
    owners_ref,
    mine_ref,
    top_ref,
    in_sem,
    out_sem,
):
    copies = fetch(
        (
            (packed_hbm.at[:, pl.ds(0, SRC_ROWS)], sources_ref),
            (packed_hbm.at[:, pl.ds(SRC_ROWS, BASIS_ROWS)], basis_ref),
            (packed_hbm.at[:, pl.ds(OWNER_ROW, 16)], owners_ref),
            (packed_hbm.at[:, pl.ds(TOP_ROW, RANK)], matrix_hbm),
        ),
        in_sem,
    )
    copies[0].wait()
    for g in range(LEAVES // 4):
        tiles = [sources_ref[s, g * RHS : (g + 1) * RHS, :] for s in range(SLABS)]
        for i in range(4):
            mine_ref[4 * g + i] = jnp.concatenate(
                [t[:, i * PART : (i + 1) * PART] for t in tiles], axis=1
            )
    rows = pl.ds(0, LEAVES)
    out_rows = pltpu.make_async_copy(mine_ref.at[rows], mine_hbm.at[rows], out_sem.at[0])
    out_rows.start()
    copies[1].wait()
    pairs = []
    for i in range(LEAVES // 2):
        basis = jnp.concatenate(
            [basis_ref[s, i * PART : (i + 1) * PART, :] for s in range(SLABS)], axis=0
        )
        pairs.append(leaf_pair([mine_ref[2 * i], mine_ref[2 * i + 1]], basis))

    def keep(i, parts):
        mine_ref[LEAVES + i] = jnp.concatenate(parts, axis=1)

    top = climb(pairs, transfer_ref, keep).astype(bf16)
    rows = pl.ds(LEAVES, PAIRS)
    out_pairs = pltpu.make_async_copy(mine_ref.at[rows], mine_hbm.at[rows], out_sem.at[1])
    out_pairs.start()
    row = jnp.concatenate([top[: RHS // 2], top[RHS // 2 :]], axis=1)
    top_ref[...] = jnp.broadcast_to(row[None], top_ref.shape)
    out_top = pltpu.make_async_copy(top_ref, top_hbm, out_sem.at[2])
    out_top.start()
    copies[2].wait()
    for s in range(SLABS):
        owner_ref[s : s + 1, :] = owners_ref[s].astype(f32)[:1].astype(jnp.int32)
    out_rows.wait()
    out_pairs.wait()
    out_top.wait()
    copies[3].wait()


def top_kernel(
    owner_hbm, tops_hbm, matrix_hbm, transfer_ref, out_ref, owner_ref, tops_ref, matrix_ref, in_sem
):
    copies = fetch(
        (
            (tops_hbm, tops_ref),
            (matrix_hbm, matrix_ref),
            (owner_hbm, owner_ref),
        ),
        in_sem,
    )
    for copy in copies:
        copy.wait()

    def top_of(s, e):
        block = tops_ref[owner_ref[s, e]]
        return jnp.concatenate([block[:, :RANK], block[:, RANK:]], axis=0)

    top = jnp.zeros((RHS, RANK), f32)
    for s in range(SLABS):
        picked = jnp.concatenate([top_of(s, 0), top_of(s, 1)], axis=1)
        top = top + dot(picked, matrix_ref[s], NT)
    matrices = split(pair_matrices(transfer_ref, PAIRS - 1))
    level = descend([dot3(split(top), matrices, NN)], transfer_ref, None)
    for i in range(LEAVES // 2):
        out_ref[i] = level[i]


def field_kernel(
    list_hbm,
    mine_hbm,
    received_hbm,
    swapped_hbm,
    transfer_ref,
    coupling_ref,
    leaf_hbm,
    list_ref,
    window_ref,
    leaf_ref,
    in_sem,
    out_sem,
):
    copies = fetch(
        [
            (hbm.at[pl.ds(LEAVES, PAIRS)], window_ref.at[pl.ds(k * PAIRS, PAIRS)])
            for k, hbm in zip(window_places(), (mine_hbm, received_hbm, swapped_hbm))
        ]
        + [(list_hbm, list_ref)],
        in_sem,
    )
    left = lax.broadcasted_iota(jnp.int32, (RHS, 128), 1) < RANK
    first_cluster = morton_index() * CLUSTERS - CLUSTERS
    for copy in copies:
        copy.wait()

    def swapped(x):
        return jnp.concatenate([x[:, RANK:], x[:, :RANK]], axis=1)

    def pick(g, e):
        local = list_ref[e, g] - first_cluster
        owner = (local >= CLUSTERS).astype(jnp.int32) + (local >= 2 * CLUSTERS).astype(
            jnp.int32
        )
        cluster = local - owner * CLUSTERS
        pair = lax.shift_right_logical(cluster, 1)
        block = window_ref[owner * PAIRS + pair]
        high, low = block[:, :128], block[:, 128:]
        here = (cluster - 2 * pair) == e
        return jnp.where(here, high, swapped(high)), jnp.where(here, low, swapped(low))

    def coupled(g):
        matrices = split(
            jnp.concatenate([coupling_ref[g, 0], coupling_ref[g, 1]], axis=1)
        )
        (high0, low0), (high1, low1) = pick(g, 0), pick(g, 1)
        picked = (jnp.where(left, high0, high1), jnp.where(left, low0, low1))
        return dot3(picked, matrices, NT)

    def own(i):
        return jnp.concatenate([coupled(2 * i), coupled(2 * i + 1)], axis=1)

    level = descend([own(PAIRS - 1)], transfer_ref, own)
    for i in range(LEAVES // 2):
        leaf_ref[i * RHS : (i + 1) * RHS, :] = level[i].astype(bf16)
    for copy in fetch([(leaf_ref, leaf_hbm.at[s]) for s in range(SLABS)], out_sem):
        copy.wait()


def near_kernel(
    scale_hbm,
    target_hbm,
    source_hbm,
    count_hbm,
    mine_hbm,
    received_hbm,
    swapped_hbm,
    near_hbm,
    out_ref,
    scale_ref,
    target_ref,
    source_ref,
    count_ref,
    window_ref,
    near_ref,
    product_ref,
    in_sem,
):
    chunk = near_ref.shape[0] // NEAR_CHUNKS
    copies = fetch(
        [
            (scale_hbm, scale_ref),
            (target_hbm, target_ref),
            (source_hbm, source_ref),
            (count_hbm, count_ref),
        ]
        + [
            (hbm.at[pl.ds(0, LEAVES)], window_ref.at[pl.ds(k * LEAVES, LEAVES)])
            for k, hbm in zip(window_places(), (mine_hbm, received_hbm, swapped_hbm))
        ]
        + [
            (near_hbm.at[pl.ds(k * chunk, chunk)], near_ref.at[pl.ds(k * chunk, chunk)])
            for k in range(NEAR_CHUNKS)
        ],
        in_sem,
    )
    out_ref[...] = jnp.zeros_like(out_ref)
    morton = morton_index()
    first_source = (morton - 1) * LEAVES
    first_target = morton * LEAVES
    for copy in copies[:-NEAR_CHUNKS]:
        copy.wait()
    live = count_ref[0]

    def tile(t, carry):
        base = t * TILE_SLOTS
        for k in range(TILE_SLOTS):
            slot = base + k
            row = source_ref[slot] - first_source
            product_ref[k] = dot(window_ref[row], near_ref[slot], NT)
        for k in range(TILE_SLOTS):
            slot = base + k
            target = target_ref[slot] - first_target
            weight = jnp.where(slot < live, scale_ref[slot], 0.0)
            out_ref[target] += weight * product_ref[k]
        return carry

    tiles = (live + TILE_SLOTS - 1) // TILE_SLOTS
    step = chunk // TILE_SLOTS
    for k in range(NEAR_CHUNKS):
        copies[k - NEAR_CHUNKS].wait()
        lax.fori_loop(k * step, jnp.clip(tiles, k * step, (k + 1) * step), tile, 0)


def far_kernel(parts_hbm, extra_ref, basis_ref, near_ref, out_ref, parts_ref, sem):
    half = LEAVES // 4 * RHS
    copies = fetch(
        [
            (parts_hbm.at[:, pl.ds(k * half, half)], parts_ref.at[:, pl.ds(k * half, half)])
            for k in range(2)
        ],
        sem,
    )
    for i in range(LEAVES // 2):
        if i % (LEAVES // 4) == 0:
            copies[i // (LEAVES // 4)].wait()
        rows = pl.ds(i * RHS, RHS)
        total = extra_ref[i]
        for s in range(SLABS):
            total = total + parts_ref[s, rows, :].astype(f32)
        high, low = split(total)
        both = jnp.concatenate([high, low], axis=0)
        for k in range(2):
            leaf = 2 * i + k
            product = dot(both[:, k * RANK : (k + 1) * RANK], basis_ref[leaf], NT)
            out_ref[leaf] = near_ref[leaf] + (product[:RHS] + product[RHS:])


def window_places():
    odd = lax.axis_index("slab") % 2
    return 1, 2 * odd, 2 - 2 * odd


def morton_index():
    return lax.axis_index(("z", "y"))


def vmem(n):
    return [pl.BlockSpec(memory_space=pltpu.VMEM)] * n


def smem(n):
    return [pl.BlockSpec(memory_space=pltpu.SMEM)] * n


def hbm(n):
    return [pl.BlockSpec(memory_space=pltpu.HBM)] * n


def shards(
    sources,
    basis_in,
    basis_out,
    transfer,
    coupling,
    coupling_list,
    near_block,
    near_scale,
    near_target,
    near_source,
    near_count,
):
    height, columns = lax.axis_size("z"), lax.axis_size("y")
    count = height * columns
    slots = near_block.shape[0]
    listed = coupling_list.T
    dma = pltpu.SemaphoreType.DMA

    def call(kernel, name, outs, in_specs, out_specs, scratch, limit=40, **params):
        return pl.pallas_call(
            kernel,
            out_shape=tuple(
                out[2](*out[:2]) if out[2:] else jax.ShapeDtypeStruct(*out)
                for out in outs
            ),
            in_specs=in_specs,
            out_specs=tuple(out_specs),
            scratch_shapes=scratch,
            compiler_params=pltpu.CompilerParams(vmem_limit_bytes=limit * MIB),
            name=name,
            **params,
        )

    (packed,) = call(
        pack_kernel,
        "pack",
        [((PACKED, 128), bf16)],
        hbm(4),
        vmem(1),
        [
            pltpu.VMEM(sources.shape, bf16),
            pltpu.VMEM((LEAVES, PART, RANK), bf16),
            pltpu.VMEM(coupling.shape[1:], f32),
            pltpu.SMEM(listed.shape, jnp.int32),
            dma((4,)),
        ],
        limit=56,
    )(
        pin(listed, HBM),
        pin(sources, HBM),
        pin(jnp.swapaxes(basis_in, 1, 2), HBM),
        pin(coupling, HBM),
    )
    gathered = lax.all_gather(packed, "slab")
    mine, top, matrix, owner = call(
        up_kernel,
        "up",
        [
            ((LEAVES + PAIRS, RHS, POINTS), bf16, HBM),
            ((count, RHS // 2, 128), bf16, HBM),
            ((SLABS, RANK, 128), bf16, HBM),
            ((SLABS, 128), jnp.int32),
        ],
        hbm(1) + vmem(1),
        hbm(3) + vmem(1),
        [
            pltpu.VMEM((SLABS, SRC_ROWS, 128), bf16),
            pltpu.VMEM((SLABS, BASIS_ROWS, 128), bf16),
            pltpu.VMEM((SLABS, 16, 128), bf16),
            pltpu.VMEM((LEAVES + PAIRS, RHS, POINTS), bf16),
            pltpu.VMEM((count, RHS // 2, 128), bf16),
            dma((4,)),
            dma((3,)),
        ],
    )(gathered, transfer)
    moves = []
    for m in range(count):
        for s in range(SLABS):
            to = m + 1 - 2 * (s % 2)
            if 0 <= to < count:
                moves.append((m * SLABS + s, to * SLABS + s))
    received = lax.ppermute(mine, ("z", "y", "slab"), moves)
    swapped = lax.ppermute(received, "slab", [(s, s ^ 1) for s in range(SLABS)])
    mine, received, swapped = pin(mine, HBM), pin(received, HBM), pin(swapped, HBM)
    tops = lax.all_to_all(top, ("z", "y"), 0, 0)
    (leaf,) = call(
        field_kernel,
        "field",
        [
            ((SLABS, LEAVES // 2 * RHS, 128), bf16, HBM),
        ],
        hbm(4) + vmem(2),
        hbm(1),
        [
            pltpu.SMEM(listed.shape, jnp.int32),
            pltpu.VMEM((3 * PAIRS, RHS, 256), bf16),
            pltpu.VMEM((LEAVES // 2 * RHS, 128), bf16),
            dma((4,)),
            dma((SLABS,)),
        ],

    )(
        listed,
        mine,
        received,
        swapped,
        transfer,
        coupling,
    )
    parts = lax.all_to_all(leaf, "slab", 0, 0)
    (near,) = call(
        near_kernel,
        "near",
        [((LEAVES, RHS, PART), f32)],
        hbm(8),
        vmem(1),
        [
            pltpu.SMEM((slots,), f32),
            pltpu.SMEM((slots,), jnp.int32),
            pltpu.SMEM((slots,), jnp.int32),
            pltpu.SMEM((1,), jnp.int32),
            pltpu.VMEM((3 * LEAVES, RHS, POINTS), bf16),
            pltpu.VMEM((slots, PART, POINTS), bf16),
            pltpu.VMEM((TILE_SLOTS, RHS, PART), f32),
            dma((7 + NEAR_CHUNKS,)),
        ],
    )(
        near_scale,
        near_target,
        near_source,
        near_count,
        mine,
        received,
        swapped,
        pin(near_block, HBM),
    )
    (extra,) = call(
        top_kernel,
        "top",
        [((LEAVES // 2, RHS, 128), f32)],
        hbm(3) + vmem(1),
        vmem(1),
        [
            pltpu.SMEM((SLABS, 128), jnp.int32),
            pltpu.VMEM((count, RHS // 2, 128), bf16),
            pltpu.VMEM((SLABS, RANK, 128), bf16),
            dma((3,)),
        ],
    )(owner, tops, matrix, transfer)
    (out,) = call(
        far_kernel,
        "far",
        [((LEAVES, RHS, PART), f32)],
        hbm(1) + vmem(3),
        vmem(1),
        [pltpu.VMEM((SLABS, LEAVES // 2 * RHS, 128), bf16), dma((2,))],
    )(parts, extra, jnp.swapaxes(basis_out, 1, 2), near)
    return out


COLUMNS = 8


def solution(mesh):
    grid = mesh.devices.reshape(-1, COLUMNS, mesh.shape["slab"])
    morton = ("z", "y")
    return jax.shard_map(
        shards,
        mesh=Mesh(grid, ("z", "y", "slab")),
        in_specs=(
            P(morton, None, "slab"),
            P(morton, None, "slab"),
            P(morton, None, "slab"),
            P(morton, None, None),
            P(morton, "slab", None, None),
            P(morton, "slab"),
            P(morton, "slab", None),
            P(morton),
            P(morton),
            P(morton),
            P(morton),
        ),
        out_specs=P(morton, None, "slab"),
        check_vma=False,
    )
```

```python
import jax
import jax.numpy as jnp
from jax import lax
from jax.experimental import pallas as pl
from jax.experimental.pallas import tpu as pltpu
from jax.sharding import Mesh, PartitionSpec as P

LEAVES = 16
CLUSTERS = 31
RANK = 64
RHS = 32
POINTS = 256
SLABS = 8
PART = POINTS // SLABS
PAIRS = 15
HALF = 15
LEVELS = ((0, 8), (16, 4), (24, 2), (28, 1))
SRC_ROWS = LEAVES * RHS * PART // 128
BASIS_ROWS = LEAVES * PART * RANK // 128
TOP_ROW = SRC_ROWS + BASIS_ROWS
OWNER_ROW = TOP_ROW + RANK
PACKED = OWNER_ROW + 16
TILE_SLOTS = 8
NEAR_CHUNKS = 4
bf16 = jnp.bfloat16
f32 = jnp.float32
MIB = 1024 * 1024
pin = pltpu.with_memory_space_constraint
HBM = pltpu.HBM
NT = (((1,), (1,)), ((), ()))
NN = (((1,), (0,)), ((), ()))


def dot(a, b, dims):
    return lax.dot_general(a, b, dims, preferred_element_type=f32)


def split(x):
    high = x.astype(bf16)
    return high, (x - high.astype(f32)).astype(bf16)


def dot3(a, b, dims):
    a_high, a_low = a
    b_high, b_low = b
    rows = a_high.shape[0]
    both = dot(jnp.concatenate([a_high, a_low], axis=0), b_high, dims)
    return both[:rows] + both[rows:] + dot(a_high, b_low, dims)


def pair_matrices(transfer_ref, i):
    return jnp.concatenate([transfer_ref[2 * i], transfer_ref[2 * i + 1]], axis=1)


def climb(pairs, transfer_ref, keep):
    first = 0
    count = LEAVES // 2
    while True:
        parents = []
        for i in range(first, first + count):
            parts = split(pairs[i])
            keep(i, parts)
            parents.append(dot3(parts, split(pair_matrices(transfer_ref, i)), NT))
        if count == 1:
            return parents[0]
        first = first + count
        count = count // 2
        for i in range(count):
            pairs.append(jnp.concatenate([parents[2 * i], parents[2 * i + 1]], axis=1))


def descend(level, transfer_ref):
    first = PAIRS - 1
    while first > 0:
        parents = []
        for pair in level:
            parents.append(pair[:, :RANK])
            parents.append(pair[:, RANK:])
        first = first - len(parents)
        level = []
        for i, parent in enumerate(parents):
            passed = dot3(split(parent), split(pair_matrices(transfer_ref, first + i)), NN)
            level.append(passed)
    return level


def leaf_pair(sources, basis):
    product = dot(jnp.concatenate(sources, axis=0), basis, NN)
    left = lax.broadcasted_iota(jnp.int32, (RHS, 128), 1) < RANK
    return jnp.where(left, product[:RHS], product[RHS:])


def fetch(pairs, sems):
    copies = [
        pltpu.make_async_copy(src, dst, sems.at[k]) for k, (src, dst) in enumerate(pairs)
    ]
    for copy in copies:
        copy.start()
    return copies


def pack_kernel(
    list_hbm,
    sources_hbm,
    basis_hbm,
    coupling_hbm,
    out_hbm,
    share_hbm,
    out_ref,
    share_ref,
    sources_ref,
    basis_ref,
    coupling_ref,
    half_ref,
    list_ref,
    in_sem,
    half_sem,
    out_sem,
):
    copies = fetch(
        (
            (sources_hbm, sources_ref),
            (basis_hbm, basis_ref),
            (coupling_hbm.at[CLUSTERS - 1], coupling_ref),
            (list_hbm, list_ref),
        ),
        in_sem,
    )
    halves = fetch(
        [
            (coupling_hbm.at[pl.ds(source, count)], half_ref.at[pl.ds(place, count)])
            for place, source, count in half_of(1 - lax.axis_index("slab") % 2)
        ],
        half_sem,
    )
    for copy in copies:
        copy.wait()
    for g in range(LEAVES // 4):
        out_ref[g * RHS : (g + 1) * RHS, :] = jnp.concatenate(
            [sources_ref[4 * g + i] for i in range(4)], axis=1
        )
    for i in range(LEAVES // 2):
        start = SRC_ROWS + i * PART
        out_ref[start : start + PART, :] = jnp.concatenate(
            [basis_ref[2 * i], basis_ref[2 * i + 1]], axis=1
        )
    out_ref[TOP_ROW : TOP_ROW + RANK, :] = jnp.concatenate(
        [coupling_ref[0], coupling_ref[1]], axis=1
    ).astype(bf16)
    row = lax.broadcasted_iota(jnp.int32, (16, 128), 0)
    lane = lax.broadcasted_iota(jnp.int32, (16, 128), 1)
    first_cluster = morton_index() * CLUSTERS - CLUSTERS
    listed = jnp.zeros((16, 128), jnp.int32)
    for e in range(2):
        owner = lax.shift_right_logical(list_ref[e, CLUSTERS - 1] * 2115, 16)
        listed = jnp.where((row == 0) & (lane == e), owner, listed)
        here = row == 1 + e
        for g in range(CLUSTERS - 1):
            listed = jnp.where(here & (lane == g), list_ref[e, g] - first_cluster, listed)
    out_ref[OWNER_ROW : OWNER_ROW + 16, :] = listed.astype(f32).astype(bf16)
    out = pltpu.make_async_copy(out_ref, out_hbm, out_sem.at[0])
    out.start()
    for copy in halves:
        copy.wait()
    for i in range(HALF):
        share_ref[i] = jnp.concatenate([half_ref[i, 0], half_ref[i, 1]], axis=1)
    share = pltpu.make_async_copy(share_ref, share_hbm, out_sem.at[1])
    share.start()
    out.wait()
    share.wait()


def up_kernel(
    packed_hbm,
    transfer_ref,
    mine_hbm,
    top_hbm,
    matrix_hbm,
    owner_ref,
    sources_ref,
    basis_ref,
    owners_ref,
    mine_ref,
    top_ref,
    in_sem,
    out_sem,
):
    copies = fetch(
        (
            (packed_hbm.at[:, pl.ds(0, SRC_ROWS)], sources_ref),
            (packed_hbm.at[:, pl.ds(SRC_ROWS, BASIS_ROWS)], basis_ref),
            (packed_hbm.at[:, pl.ds(OWNER_ROW, 16)], owners_ref),
            (packed_hbm.at[:, pl.ds(TOP_ROW, RANK)], matrix_hbm),
        ),
        in_sem,
    )
    copies[0].wait()
    for g in range(LEAVES // 4):
        tiles = [sources_ref[s, g * RHS : (g + 1) * RHS, :] for s in range(SLABS)]
        for i in range(4):
            mine_ref[4 * g + i] = jnp.concatenate(
                [t[:, i * PART : (i + 1) * PART] for t in tiles], axis=1
            )
    rows = pl.ds(0, LEAVES)
    out_rows = pltpu.make_async_copy(mine_ref.at[rows], mine_hbm.at[rows], out_sem.at[0])
    out_rows.start()
    copies[1].wait()
    pairs = []
    for i in range(LEAVES // 2):
        basis = jnp.concatenate(
            [basis_ref[s, i * PART : (i + 1) * PART, :] for s in range(SLABS)], axis=0
        )
        pairs.append(leaf_pair([mine_ref[2 * i], mine_ref[2 * i + 1]], basis))

    def keep(i, parts):
        mine_ref[LEAVES + i] = jnp.concatenate(parts, axis=1)

    top = climb(pairs, transfer_ref, keep).astype(bf16)
    rows = pl.ds(LEAVES, PAIRS)
    out_pairs = pltpu.make_async_copy(mine_ref.at[rows], mine_hbm.at[rows], out_sem.at[1])
    out_pairs.start()
    row = jnp.concatenate([top[: RHS // 2], top[RHS // 2 :]], axis=1)
    top_ref[...] = jnp.broadcast_to(row[None], top_ref.shape)
    out_top = pltpu.make_async_copy(top_ref, top_hbm, out_sem.at[2])
    out_top.start()
    copies[2].wait()
    for s in range(SLABS):
        owner_ref[s : s + 1, :] = owners_ref[s].astype(f32)[:1].astype(jnp.int32)
    other = owners_ref[lax.axis_index("slab") ^ 1].astype(f32)
    owner_ref[SLABS : 2 * SLABS, :] = other[:SLABS].astype(jnp.int32)
    out_rows.wait()
    out_pairs.wait()
    out_top.wait()
    copies[3].wait()


def top_kernel(
    owner_hbm, tops_hbm, matrix_hbm, transfer_ref, out_ref, owner_ref, tops_ref, matrix_ref, in_sem
):
    copies = fetch(
        (
            (tops_hbm, tops_ref),
            (matrix_hbm, matrix_ref),
            (owner_hbm.at[pl.ds(0, SLABS)], owner_ref),
        ),
        in_sem,
    )
    for copy in copies:
        copy.wait()

    def top_of(s, e):
        block = tops_ref[owner_ref[s, e]]
        return jnp.concatenate([block[:, :RANK], block[:, RANK:]], axis=0)

    top = jnp.zeros((RHS, RANK), f32)
    for s in range(SLABS):
        picked = jnp.concatenate([top_of(s, 0), top_of(s, 1)], axis=1)
        top = top + dot(picked, matrix_ref[s], NT)
    matrices = split(pair_matrices(transfer_ref, PAIRS - 1))
    level = descend([dot3(split(top), matrices, NN)], transfer_ref)
    for i in range(LEAVES // 2):
        out_ref[i] = level[i]


def half_of(half):
    place = 0
    runs = []
    for first, count in LEVELS:
        runs.append((place, first + half * count, count))
        place += count
    return runs


def field_kernel(
    list_hbm,
    other_hbm,
    mine_hbm,
    received_hbm,
    swapped_hbm,
    share_hbm,
    transfer_ref,
    coupling_ref,
    leaf_hbm,
    list_ref,
    other_ref,
    window_ref,
    share_ref,
    leaf_ref,
    in_sem,
    out_sem,
):
    copies = fetch(
        [
            (hbm.at[pl.ds(LEAVES, PAIRS)], window_ref.at[pl.ds(k * PAIRS, PAIRS)])
            for k, hbm in zip(window_places(), (mine_hbm, received_hbm, swapped_hbm))
        ]
        + [
            (list_hbm, list_ref),
            (other_hbm.at[pl.ds(SLABS, SLABS)], other_ref),
            (share_hbm, share_ref),
        ],
        in_sem,
    )
    half = lax.axis_index("slab") % 2
    left = lax.broadcasted_iota(jnp.int32, (RHS, 128), 1) < RANK
    first_cluster = morton_index() * CLUSTERS - CLUSTERS
    for copy in copies:
        copy.wait()

    def swapped(x):
        return jnp.concatenate([x[:, RANK:], x[:, :RANK]], axis=1)

    def pick(local, e):
        owner = (local >= CLUSTERS).astype(jnp.int32) + (local >= 2 * CLUSTERS).astype(
            jnp.int32
        )
        cluster = local - owner * CLUSTERS
        pair = lax.shift_right_logical(cluster, 1)
        block = window_ref[owner * PAIRS + pair]
        high, low = block[:, :128], block[:, 128:]
        here = (cluster - 2 * pair) == e
        return jnp.where(here, high, swapped(high)), jnp.where(here, low, swapped(low))

    def pick_two(locals_of):
        (high0, low0), (high1, low1) = pick(locals_of(0), 0), pick(locals_of(1), 1)
        return jnp.where(left, high0, high1), jnp.where(left, low0, low1)

    def coupled(place, g):
        own = pick_two(lambda e: list_ref[e, g] - first_cluster)
        other = pick_two(lambda e: other_ref[1 + e, g])
        picked = [jnp.concatenate([x, y], axis=1) for x, y in zip(own, other)]
        matrices = jnp.concatenate(
            [coupling_ref[g, 0], coupling_ref[g, 1], share_ref[place]], axis=1
        )
        return dot3(picked, split(matrices), NT)

    runs = half_of(half)
    place, g, _ = runs[-1]
    level = [coupled(place, g)]
    for place, first, count in reversed(runs[:-1]):
        parents, level = level, []
        for i, parent in enumerate(parents):
            own = [coupled(place + 2 * i + k, first + 2 * i + k) for k in range(2)]
            pair = lax.shift_right_logical(first, 1) + i
            passed = dot3(split(parent), split(pair_matrices(transfer_ref, pair)), NN)
            total = jnp.concatenate(own, axis=1) + passed
            level += [total] if count == LEAVES // 2 else [total[:, :RANK], total[:, RANK:]]
    for i in range(LEAVES // 4):
        leaf_ref[i * RHS : (i + 1) * RHS, :] = level[i].astype(bf16)
    for copy in fetch([(leaf_ref, leaf_hbm.at[s]) for s in range(SLABS)], out_sem):
        copy.wait()


def near_kernel(
    scale_hbm,
    target_hbm,
    source_hbm,
    count_hbm,
    mine_hbm,
    received_hbm,
    swapped_hbm,
    near_hbm,
    out_ref,
    scale_ref,
    target_ref,
    source_ref,
    count_ref,
    window_ref,
    near_ref,
    product_ref,
    in_sem,
):
    chunk = near_ref.shape[0] // NEAR_CHUNKS
    copies = fetch(
        [
            (scale_hbm, scale_ref),
            (target_hbm, target_ref),
            (source_hbm, source_ref),
            (count_hbm, count_ref),
        ]
        + [
            (hbm.at[pl.ds(0, LEAVES)], window_ref.at[pl.ds(k * LEAVES, LEAVES)])
            for k, hbm in zip(window_places(), (mine_hbm, received_hbm, swapped_hbm))
        ]
        + [
            (near_hbm.at[pl.ds(k * chunk, chunk)], near_ref.at[pl.ds(k * chunk, chunk)])
            for k in range(NEAR_CHUNKS)
        ],
        in_sem,
    )
    out_ref[...] = jnp.zeros_like(out_ref)
    morton = morton_index()
    first_source = (morton - 1) * LEAVES
    first_target = morton * LEAVES
    for copy in copies[:-NEAR_CHUNKS]:
        copy.wait()
    live = count_ref[0]

    def tile(t, carry):
        base = t * TILE_SLOTS
        for k in range(TILE_SLOTS):
            slot = base + k
            row = source_ref[slot] - first_source
            product_ref[k] = dot(window_ref[row], near_ref[slot], NT)
        for k in range(TILE_SLOTS):
            slot = base + k
            target = target_ref[slot] - first_target
            weight = jnp.where(slot < live, scale_ref[slot], 0.0)
            out_ref[target] += weight * product_ref[k]
        return carry

    tiles = (live + TILE_SLOTS - 1) // TILE_SLOTS
    step = chunk // TILE_SLOTS
    for k in range(NEAR_CHUNKS):
        copies[k - NEAR_CHUNKS].wait()
        lax.fori_loop(k * step, jnp.clip(tiles, k * step, (k + 1) * step), tile, 0)


def far_kernel(parts_hbm, extra_ref, basis_ref, near_ref, out_ref, parts_ref, sem):
    copies = fetch([(parts_hbm, parts_ref)], sem)
    copies[0].wait()
    for i in range(LEAVES // 2):
        half, place = divmod(i, LEAVES // 4)
        rows = pl.ds(place * RHS, RHS)
        total = extra_ref[i]
        for s in range(half, SLABS, 2):
            total = total + parts_ref[s, rows, :].astype(f32)
        high, low = split(total)
        both = jnp.concatenate([high, low], axis=0)
        for k in range(2):
            leaf = 2 * i + k
            product = dot(both[:, k * RANK : (k + 1) * RANK], basis_ref[leaf], NT)
            out_ref[leaf] = near_ref[leaf] + (product[:RHS] + product[RHS:])


def window_places():
    odd = lax.axis_index("slab") % 2
    return 1, 2 * odd, 2 - 2 * odd


def morton_index():
    return lax.axis_index(("z", "y"))


def vmem(n):
    return [pl.BlockSpec(memory_space=pltpu.VMEM)] * n


def smem(n):
    return [pl.BlockSpec(memory_space=pltpu.SMEM)] * n


def hbm(n):
    return [pl.BlockSpec(memory_space=pltpu.HBM)] * n


def shards(
    sources,
    basis_in,
    basis_out,
    transfer,
    coupling,
    coupling_list,
    near_block,
    near_scale,
    near_target,
    near_source,
    near_count,
):
    height, columns = lax.axis_size("z"), lax.axis_size("y")
    count = height * columns
    slots = near_block.shape[0]
    listed = coupling_list.T
    dma = pltpu.SemaphoreType.DMA

    def call(kernel, name, outs, in_specs, out_specs, scratch, limit=40, **params):
        return pl.pallas_call(
            kernel,
            out_shape=tuple(
                out[2](*out[:2]) if out[2:] else jax.ShapeDtypeStruct(*out)
                for out in outs
            ),
            in_specs=in_specs,
            out_specs=tuple(out_specs),
            scratch_shapes=scratch,
            compiler_params=pltpu.CompilerParams(vmem_limit_bytes=limit * MIB),
            name=name,
            **params,
        )

    packed, share = call(
        pack_kernel,
        "pack",
        [((PACKED, 128), bf16, HBM), ((HALF, RANK, 128), f32, HBM)],
        hbm(4),
        hbm(2),
        [
            pltpu.VMEM((PACKED, 128), bf16),
            pltpu.VMEM((HALF, RANK, 128), f32),
            pltpu.VMEM(sources.shape, bf16),
            pltpu.VMEM((LEAVES, PART, RANK), bf16),
            pltpu.VMEM(coupling.shape[1:], f32),
            pltpu.VMEM((HALF, *coupling.shape[1:]), f32),
            pltpu.SMEM(listed.shape, jnp.int32),
            dma((4,)),
            dma((len(LEVELS),)),
            dma((2,)),
        ],
    )(
        pin(listed, HBM),
        pin(sources, HBM),
        pin(jnp.swapaxes(basis_in, 1, 2), HBM),
        pin(coupling, HBM),
    )
    gathered = lax.all_gather(packed, "slab")
    mine, top, matrix, owner = call(
        up_kernel,
        "up",
        [
            ((LEAVES + PAIRS, RHS, POINTS), bf16, HBM),
            ((count, RHS // 2, 128), bf16, HBM),
            ((SLABS, RANK, 128), bf16, HBM),
            ((2 * SLABS, 128), jnp.int32),
        ],
        hbm(1) + vmem(1),
        hbm(3) + vmem(1),
        [
            pltpu.VMEM((SLABS, SRC_ROWS, 128), bf16),
            pltpu.VMEM((SLABS, BASIS_ROWS, 128), bf16),
            pltpu.VMEM((SLABS, 16, 128), bf16),
            pltpu.VMEM((LEAVES + PAIRS, RHS, POINTS), bf16),
            pltpu.VMEM((count, RHS // 2, 128), bf16),
            dma((4,)),
            dma((3,)),
        ],
    )(gathered, transfer)
    moves = []
    for m in range(count):
        for s in range(SLABS):
            to = m + 1 - 2 * (s % 2)
            if 0 <= to < count:
                moves.append((m * SLABS + s, to * SLABS + s))
    received = lax.ppermute(mine, ("z", "y", "slab"), moves)
    swapped = lax.ppermute(received, "slab", [(s, s ^ 1) for s in range(SLABS)])
    share = lax.ppermute(share, "slab", [(s, s ^ 1) for s in range(SLABS)])
    mine, received, swapped = pin(mine, HBM), pin(received, HBM), pin(swapped, HBM)
    tops = lax.all_to_all(top, ("z", "y"), 0, 0)
    (leaf,) = call(
        field_kernel,
        "field",
        [((SLABS, LEAVES // 4 * RHS, 128), bf16, HBM)],
        hbm(6) + vmem(2),
        hbm(1),
        [
            pltpu.SMEM(listed.shape, jnp.int32),
            pltpu.SMEM((SLABS, 128), jnp.int32),
            pltpu.VMEM((3 * PAIRS, RHS, 256), bf16),
            pltpu.VMEM((HALF, RANK, 128), f32),
            pltpu.VMEM((LEAVES // 4 * RHS, 128), bf16),
            dma((6,)),
            dma((SLABS,)),
        ],
    )(listed, owner, mine, received, swapped, pin(share, HBM), transfer, coupling)
    parts = lax.all_to_all(leaf, "slab", 0, 0)
    (near,) = call(
        near_kernel,
        "near",
        [((LEAVES, RHS, PART), f32)],
        hbm(8),
        vmem(1),
        [
            pltpu.SMEM((slots,), f32),
            pltpu.SMEM((slots,), jnp.int32),
            pltpu.SMEM((slots,), jnp.int32),
            pltpu.SMEM((1,), jnp.int32),
            pltpu.VMEM((3 * LEAVES, RHS, POINTS), bf16),
            pltpu.VMEM((slots, PART, POINTS), bf16),
            pltpu.VMEM((TILE_SLOTS, RHS, PART), f32),
            dma((7 + NEAR_CHUNKS,)),
        ],
    )(
        near_scale,
        near_target,
        near_source,
        near_count,
        mine,
        received,
        swapped,
        pin(near_block, HBM),
    )
    (extra,) = call(
        top_kernel,
        "top",
        [((LEAVES // 2, RHS, 128), f32)],
        hbm(3) + vmem(1),
        vmem(1),
        [
            pltpu.SMEM((SLABS, 128), jnp.int32),
            pltpu.VMEM((count, RHS // 2, 128), bf16),
            pltpu.VMEM((SLABS, RANK, 128), bf16),
            dma((3,)),
        ],
    )(owner, tops, matrix, transfer)
    (out,) = call(
        far_kernel,
        "far",
        [((LEAVES, RHS, PART), f32)],
        hbm(1) + vmem(3),
        vmem(1),
        [pltpu.VMEM((SLABS, LEAVES // 4 * RHS, 128), bf16), dma((1,))],
    )(parts, extra, jnp.swapaxes(basis_out, 1, 2), near)
    return out


COLUMNS = 8


def solution(mesh):
    grid = mesh.devices.reshape(-1, COLUMNS, mesh.shape["slab"])
    morton = ("z", "y")
    return jax.shard_map(
        shards,
        mesh=Mesh(grid, ("z", "y", "slab")),
        in_specs=(
            P(morton, None, "slab"),
            P(morton, None, "slab"),
            P(morton, None, "slab"),
            P(morton, None, None),
            P(morton, "slab", None, None),
            P(morton, "slab"),
            P(morton, "slab", None),
            P(morton),
            P(morton),
            P(morton),
            P(morton),
        ),
        out_specs=P(morton, None, "slab"),
        check_vma=False,
    )
```

```python
import jax
import jax.numpy as jnp
from jax import lax
from jax.experimental import pallas as pl
from jax.experimental.pallas import tpu as pltpu
from jax.sharding import Mesh, PartitionSpec as P

LEAVES = 16
CLUSTERS = 31
RANK = 64
RHS = 32
POINTS = 256
SLABS = 8
PART = POINTS // SLABS
PAIRS = 15
HALF = 15
LEVELS = ((0, 8), (16, 4), (24, 2), (28, 1))
SRC_ROWS = LEAVES * RHS * PART // 128
BASIS_ROWS = LEAVES * PART * RANK // 128
TOP_ROW = SRC_ROWS + BASIS_ROWS
OWNER_ROW = TOP_ROW + RANK
PACKED = OWNER_ROW + 16
TILE_SLOTS = 48
NEAR_CHUNKS = 4
bf16 = jnp.bfloat16
f32 = jnp.float32
MIB = 1024 * 1024
pin = pltpu.with_memory_space_constraint
HBM = pltpu.HBM
NT = (((1,), (1,)), ((), ()))
NN = (((1,), (0,)), ((), ()))


def dot(a, b, dims):
    return lax.dot_general(a, b, dims, preferred_element_type=f32)


def split(x):
    high = x.astype(bf16)
    return high, (x - high.astype(f32)).astype(bf16)


def dot3(a, b, dims):
    a_high, a_low = a
    b_high, b_low = b
    rows = a_high.shape[0]
    both = dot(jnp.concatenate([a_high, a_low], axis=0), b_high, dims)
    return both[:rows] + both[rows:] + dot(a_high, b_low, dims)


def pair_matrices(transfer_ref, i):
    return jnp.concatenate([transfer_ref[2 * i], transfer_ref[2 * i + 1]], axis=1)


def climb(pairs, transfer_ref, keep):
    first = 0
    count = LEAVES // 2
    while True:
        parents = []
        for i in range(first, first + count):
            parts = split(pairs[i])
            keep(i, parts)
            parents.append(dot3(parts, split(pair_matrices(transfer_ref, i)), NT))
        if count == 1:
            return parents[0]
        first = first + count
        count = count // 2
        for i in range(count):
            pairs.append(jnp.concatenate([parents[2 * i], parents[2 * i + 1]], axis=1))


def descend(level, transfer_ref):
    first = PAIRS - 1
    while first > 0:
        parents = []
        for pair in level:
            parents.append(pair[:, :RANK])
            parents.append(pair[:, RANK:])
        first = first - len(parents)
        level = []
        for i, parent in enumerate(parents):
            passed = dot3(split(parent), split(pair_matrices(transfer_ref, first + i)), NN)
            level.append(passed)
    return level


def leaf_pair(sources, basis):
    product = dot(jnp.concatenate(sources, axis=0), basis, NN)
    left = lax.broadcasted_iota(jnp.int32, (RHS, 128), 1) < RANK
    return jnp.where(left, product[:RHS], product[RHS:])


def fetch(pairs, sems):
    copies = [
        pltpu.make_async_copy(src, dst, sems.at[k]) for k, (src, dst) in enumerate(pairs)
    ]
    for copy in copies:
        copy.start()
    return copies


def pack_kernel(
    list_hbm,
    sources_hbm,
    basis_hbm,
    coupling_hbm,
    out_hbm,
    share_hbm,
    out_ref,
    share_ref,
    sources_ref,
    basis_ref,
    coupling_ref,
    half_ref,
    list_ref,
    in_sem,
    half_sem,
    out_sem,
):
    copies = fetch(
        (
            (sources_hbm, sources_ref),
            (basis_hbm, basis_ref),
            (coupling_hbm.at[CLUSTERS - 1], coupling_ref),
            (list_hbm, list_ref),
        ),
        in_sem,
    )
    halves = fetch(
        [
            (coupling_hbm.at[pl.ds(source, count)], half_ref.at[pl.ds(place, count)])
            for place, source, count in half_of(1 - lax.axis_index("slab") % 2)
        ],
        half_sem,
    )
    for copy in copies:
        copy.wait()
    for g in range(LEAVES // 4):
        out_ref[g * RHS : (g + 1) * RHS, :] = jnp.concatenate(
            [sources_ref[4 * g + i] for i in range(4)], axis=1
        )
    for i in range(LEAVES // 2):
        start = SRC_ROWS + i * PART
        out_ref[start : start + PART, :] = jnp.concatenate(
            [basis_ref[2 * i], basis_ref[2 * i + 1]], axis=1
        )
    out_ref[TOP_ROW : TOP_ROW + RANK, :] = jnp.concatenate(
        [coupling_ref[0], coupling_ref[1]], axis=1
    ).astype(bf16)
    row = lax.broadcasted_iota(jnp.int32, (16, 128), 0)
    lane = lax.broadcasted_iota(jnp.int32, (16, 128), 1)
    first_cluster = morton_index() * CLUSTERS - CLUSTERS
    listed = jnp.zeros((16, 128), jnp.int32)
    for e in range(2):
        owner = lax.shift_right_logical(list_ref[e, CLUSTERS - 1] * 2115, 16)
        listed = jnp.where((row == 0) & (lane == e), owner, listed)
        here = row == 1 + e
        for g in range(CLUSTERS - 1):
            listed = jnp.where(here & (lane == g), list_ref[e, g] - first_cluster, listed)
    out_ref[OWNER_ROW : OWNER_ROW + 16, :] = listed.astype(f32).astype(bf16)
    out = pltpu.make_async_copy(out_ref, out_hbm, out_sem.at[0])
    out.start()
    for copy in halves:
        copy.wait()
    for i in range(HALF):
        share_ref[i] = jnp.concatenate([half_ref[i, 0], half_ref[i, 1]], axis=1)
    share = pltpu.make_async_copy(share_ref, share_hbm, out_sem.at[1])
    share.start()
    out.wait()
    share.wait()


def up_kernel(
    packed_ref,
    transfer_ref,
    mine_hbm,
    top_hbm,
    matrix_hbm,
    owner_ref,
    mine_ref,
    top_ref,
    out_sem,
):
    out_matrix = pltpu.make_async_copy(
        packed_ref.at[:, pl.ds(TOP_ROW, RANK)], matrix_hbm, out_sem.at[3]
    )
    out_matrix.start()
    for g in range(LEAVES // 4):
        tiles = [packed_ref[s, g * RHS : (g + 1) * RHS, :] for s in range(SLABS)]
        for i in range(4):
            mine_ref[4 * g + i] = jnp.concatenate(
                [t[:, i * PART : (i + 1) * PART] for t in tiles], axis=1
            )
    rows = pl.ds(0, LEAVES)
    out_rows = pltpu.make_async_copy(mine_ref.at[rows], mine_hbm.at[rows], out_sem.at[0])
    out_rows.start()
    pairs = []
    for i in range(LEAVES // 2):
        start = SRC_ROWS + i * PART
        basis = jnp.concatenate(
            [packed_ref[s, start : start + PART, :] for s in range(SLABS)], axis=0
        )
        pairs.append(leaf_pair([mine_ref[2 * i], mine_ref[2 * i + 1]], basis))

    def keep(i, parts):
        mine_ref[LEAVES + i] = jnp.concatenate(parts, axis=1)

    top = climb(pairs, transfer_ref, keep).astype(bf16)
    rows = pl.ds(LEAVES, PAIRS)
    out_pairs = pltpu.make_async_copy(mine_ref.at[rows], mine_hbm.at[rows], out_sem.at[1])
    out_pairs.start()
    row = jnp.concatenate([top[: RHS // 2], top[RHS // 2 :]], axis=1)
    top_ref[...] = jnp.broadcast_to(row[None], top_ref.shape)
    out_top = pltpu.make_async_copy(top_ref, top_hbm, out_sem.at[2])
    out_top.start()
    for s in range(SLABS):
        owner_ref[s : s + 1, :] = packed_ref[s, OWNER_ROW:].astype(f32)[:1].astype(jnp.int32)
    other = packed_ref[lax.axis_index("slab") ^ 1, OWNER_ROW:].astype(f32)
    owner_ref[SLABS : 2 * SLABS, :] = other[:SLABS].astype(jnp.int32)
    out_rows.wait()
    out_pairs.wait()
    out_top.wait()
    out_matrix.wait()


def half_of(half):
    place = 0
    runs = []
    for first, count in LEVELS:
        runs.append((place, first + half * count, count))
        place += count
    return runs


def field_kernel(
    list_hbm,
    other_hbm,
    mine_hbm,
    received_hbm,
    swapped_hbm,
    scale_hbm,
    target_hbm,
    source_hbm,
    count_hbm,
    near_hbm,
    share_ref,
    transfer_ref,
    coupling_ref,
    leaf_hbm,
    out_ref,
    list_ref,
    other_ref,
    window_ref,
    high_ref,
    low_ref,
    leaf_ref,
    scale_ref,
    target_ref,
    source_ref,
    count_ref,
    rows_ref,
    near_ref,
    in_sem,
    near_sem,
    out_sem,
):
    copies = fetch(
        [
            (hbm.at[pl.ds(LEAVES, PAIRS)], window_ref.at[pl.ds(k * PAIRS, PAIRS)])
            for k, hbm in zip(window_places(), (mine_hbm, received_hbm, swapped_hbm))
        ]
        + [
            (list_hbm, list_ref),
            (other_hbm.at[pl.ds(SLABS, SLABS)], other_ref),
        ],
        in_sem,
    )
    chunk = near_ref.shape[0] // NEAR_CHUNKS
    near_copies = fetch(
        [
            (scale_hbm, scale_ref),
            (target_hbm, target_ref),
            (source_hbm, source_ref),
            (count_hbm, count_ref),
        ]
        + [
            (hbm.at[pl.ds(0, LEAVES)], rows_ref.at[pl.ds(k * LEAVES, LEAVES)])
            for k, hbm in zip(window_places(), (mine_hbm, received_hbm, swapped_hbm))
        ]
        + [
            (near_hbm.at[pl.ds(k * chunk, chunk)], near_ref.at[pl.ds(k * chunk, chunk)])
            for k in range(NEAR_CHUNKS)
        ],
        near_sem,
    )
    out_ref[...] = jnp.zeros_like(out_ref)
    runs = half_of(lax.axis_index("slab") % 2)
    for start, first, count in runs:
        for i in range(count):
            matrices = jnp.concatenate(
                [coupling_ref[first + i, 0], coupling_ref[first + i, 1], share_ref[start + i]],
                axis=1,
            )
            high_ref[start + i], low_ref[start + i] = split(matrices)
    left = lax.broadcasted_iota(jnp.int32, (RHS, 128), 1) < RANK
    first_cluster = morton_index() * CLUSTERS - CLUSTERS
    for copy in copies:
        copy.wait()

    def swapped(x):
        return jnp.concatenate([x[:, RANK:], x[:, :RANK]], axis=1)

    def pick(local, e):
        owner = (local >= CLUSTERS).astype(jnp.int32) + (local >= 2 * CLUSTERS).astype(
            jnp.int32
        )
        cluster = local - owner * CLUSTERS
        pair = lax.shift_right_logical(cluster, 1)
        block = window_ref[owner * PAIRS + pair]
        high, low = block[:, :128], block[:, 128:]
        here = (cluster - 2 * pair) == e
        return jnp.where(here, high, swapped(high)), jnp.where(here, low, swapped(low))

    def pick_two(locals_of):
        (high0, low0), (high1, low1) = pick(locals_of(0), 0), pick(locals_of(1), 1)
        return jnp.where(left, high0, high1), jnp.where(left, low0, low1)

    def coupled(place, g):
        own = pick_two(lambda e: list_ref[e, g] - first_cluster)
        other = pick_two(lambda e: other_ref[1 + e, g])
        picked = [jnp.concatenate([x, y], axis=1) for x, y in zip(own, other)]
        return dot3(picked, (high_ref[place], low_ref[place]), NT)

    place, g, _ = runs[-1]
    level = [coupled(place, g)]
    for place, first, count in reversed(runs[:-1]):
        parents, level = level, []
        for i, parent in enumerate(parents):
            own = [coupled(place + 2 * i + k, first + 2 * i + k) for k in range(2)]
            pair = lax.shift_right_logical(first, 1) + i
            passed = dot3(split(parent), split(pair_matrices(transfer_ref, pair)), NN)
            total = jnp.concatenate(own, axis=1) + passed
            level += [total] if count == LEAVES // 2 else [total[:, :RANK], total[:, RANK:]]
    for i in range(LEAVES // 4):
        leaf_ref[i * RHS : (i + 1) * RHS, :] = level[i].astype(bf16)
    leaf_copies = fetch([(leaf_ref, leaf_hbm.at[s]) for s in range(SLABS)], out_sem)

    morton = morton_index()
    first_source = (morton - 1) * LEAVES
    first_target = morton * LEAVES
    for copy in near_copies[:-NEAR_CHUNKS]:
        copy.wait()
    live = count_ref[0]

    def tile(t, carry):
        base = t * TILE_SLOTS
        products = []
        for k in range(TILE_SLOTS):
            slot = base + k
            row = source_ref[slot] - first_source
            products.append(dot(rows_ref[row], near_ref[slot], NT))
        for k in range(TILE_SLOTS):
            slot = base + k
            target = target_ref[slot] - first_target
            weight = jnp.where(slot < live, scale_ref[slot], 0.0)
            out_ref[target] += weight * products[k]
        return carry

    tiles = (live + TILE_SLOTS - 1) // TILE_SLOTS
    step = chunk // TILE_SLOTS
    for k in range(NEAR_CHUNKS):
        near_copies[k - NEAR_CHUNKS].wait()
        lax.fori_loop(k * step, jnp.clip(tiles, k * step, (k + 1) * step), tile, 0)
    for copy in leaf_copies:
        copy.wait()


def top_kernel(
    owner_hbm,
    tops_hbm,
    matrix_hbm,
    transfer_ref,
    extra_ref,
    owner_ref,
    tops_ref,
    matrix_ref,
    in_sem,
):
    copies = fetch(
        (
            (owner_hbm.at[pl.ds(0, SLABS)], owner_ref),
            (tops_hbm, tops_ref),
            (matrix_hbm, matrix_ref),
        ),
        in_sem,
    )
    for copy in copies:
        copy.wait()

    def top_of(s, e):
        block = tops_ref[owner_ref[s, e]]
        return jnp.concatenate([block[:, :RANK], block[:, RANK:]], axis=0)

    top = jnp.zeros((RHS, RANK), f32)
    for s in range(SLABS):
        picked = jnp.concatenate([top_of(s, 0), top_of(s, 1)], axis=1)
        top = top + dot(picked, matrix_ref[s], NT)
    matrices = split(pair_matrices(transfer_ref, PAIRS - 1))
    level = descend([dot3(split(top), matrices, NN)], transfer_ref)
    for i in range(LEAVES // 2):
        extra_ref[i] = level[i]


def far_kernel(parts_ref, extra_ref, basis_ref, near_ref, out_ref):
    for i in range(LEAVES // 2):
        half, place = divmod(i, LEAVES // 4)
        rows = pl.ds(place * RHS, RHS)
        total = extra_ref[i]
        for s in range(half, SLABS, 2):
            total = total + parts_ref[s, rows, :].astype(f32)
        high, low = split(total)
        both = jnp.concatenate([high, low], axis=0)
        for k in range(2):
            leaf = 2 * i + k
            product = dot(both[:, k * RANK : (k + 1) * RANK], basis_ref[leaf], NT)
            out_ref[leaf] = near_ref[leaf] + (product[:RHS] + product[RHS:])


def window_places():
    odd = lax.axis_index("slab") % 2
    return 1, 2 * odd, 2 - 2 * odd


def morton_index():
    return lax.axis_index(("z", "y"))


def vmem(n):
    return [pl.BlockSpec(memory_space=pltpu.VMEM)] * n


def smem(n):
    return [pl.BlockSpec(memory_space=pltpu.SMEM)] * n


def hbm(n):
    return [pl.BlockSpec(memory_space=pltpu.HBM)] * n


def shards(
    sources,
    basis_in,
    basis_out,
    transfer,
    coupling,
    coupling_list,
    near_block,
    near_scale,
    near_target,
    near_source,
    near_count,
):
    height, columns = lax.axis_size("z"), lax.axis_size("y")
    count = height * columns
    slots = near_block.shape[0]
    listed = coupling_list.T
    dma = pltpu.SemaphoreType.DMA

    def call(kernel, name, outs, in_specs, out_specs, scratch, limit=40, **params):
        return pl.pallas_call(
            kernel,
            out_shape=tuple(
                out[2](*out[:2]) if out[2:] else jax.ShapeDtypeStruct(*out)
                for out in outs
            ),
            in_specs=in_specs,
            out_specs=tuple(out_specs),
            scratch_shapes=scratch,
            compiler_params=pltpu.CompilerParams(vmem_limit_bytes=limit * MIB),
            name=name,
            **params,
        )

    packed, share = call(
        pack_kernel,
        "pack",
        [((PACKED, 128), bf16, HBM), ((HALF, RANK, 128), f32, HBM)],
        hbm(4),
        hbm(2),
        [
            pltpu.VMEM((PACKED, 128), bf16),
            pltpu.VMEM((HALF, RANK, 128), f32),
            pltpu.VMEM(sources.shape, bf16),
            pltpu.VMEM((LEAVES, PART, RANK), bf16),
            pltpu.VMEM(coupling.shape[1:], f32),
            pltpu.VMEM((HALF, *coupling.shape[1:]), f32),
            pltpu.SMEM(listed.shape, jnp.int32),
            dma((4,)),
            dma((len(LEVELS),)),
            dma((2,)),
        ],
    )(
        pin(listed, HBM),
        pin(sources, HBM),
        pin(jnp.swapaxes(basis_in, 1, 2), HBM),
        pin(coupling, HBM),
    )
    gathered = lax.all_gather(packed, "slab")
    mine, top, matrix, owner = call(
        up_kernel,
        "up",
        [
            ((LEAVES + PAIRS, RHS, POINTS), bf16, HBM),
            ((count, RHS // 2, 128), bf16, HBM),
            ((SLABS, RANK, 128), bf16, HBM),
            ((2 * SLABS, 128), jnp.int32),
        ],
        vmem(2),
        hbm(3) + vmem(1),
        [
            pltpu.VMEM((LEAVES + PAIRS, RHS, POINTS), bf16),
            pltpu.VMEM((count, RHS // 2, 128), bf16),
            dma((4,)),
        ],
    )(pin(gathered, pltpu.VMEM), transfer)
    moves = []
    for m in range(count):
        for s in range(SLABS):
            to = m + 1 - 2 * (s % 2)
            if 0 <= to < count:
                moves.append((m * SLABS + s, to * SLABS + s))
    received = lax.ppermute(mine, ("z", "y", "slab"), moves)
    swapped = lax.ppermute(received, "slab", [(s, s ^ 1) for s in range(SLABS)])
    share = lax.ppermute(share, "slab", [(s, s ^ 1) for s in range(SLABS)])
    mine, received, swapped = pin(mine, HBM), pin(received, HBM), pin(swapped, pltpu.VMEM)
    tops = lax.all_to_all(top, ("z", "y"), 0, 0)
    leaf, near = call(
        field_kernel,
        "field",
        [((SLABS, LEAVES // 4 * RHS, 128), bf16, HBM), ((LEAVES, RHS, PART), f32)],
        hbm(10) + vmem(3),
        hbm(1) + vmem(1),
        [
            pltpu.SMEM(listed.shape, jnp.int32),
            pltpu.SMEM((SLABS, 128), jnp.int32),
            pltpu.VMEM((3 * PAIRS, RHS, 256), bf16),
            pltpu.VMEM((HALF, RANK, 256), bf16),
            pltpu.VMEM((HALF, RANK, 256), bf16),
            pltpu.VMEM((LEAVES // 4 * RHS, 128), bf16),
            pltpu.SMEM((slots,), f32),
            pltpu.SMEM((slots,), jnp.int32),
            pltpu.SMEM((slots,), jnp.int32),
            pltpu.SMEM((1,), jnp.int32),
            pltpu.VMEM((3 * LEAVES, RHS, POINTS), bf16),
            pltpu.VMEM((slots, PART, POINTS), bf16),
            dma((5,)),
            dma((7 + NEAR_CHUNKS,)),
            dma((SLABS,)),
        ],
    )(
        listed,
        owner,
        mine,
        received,
        swapped,
        pin(near_scale, HBM),
        pin(near_target, HBM),
        pin(near_source, HBM),
        near_count,
        pin(near_block, HBM),
        pin(share, pltpu.VMEM),
        transfer,
        coupling,
    )
    parts = lax.all_to_all(leaf, "slab", 0, 0)
    (extra,) = call(
        top_kernel,
        "top",
        [((LEAVES // 2, RHS, 128), f32)],
        hbm(3) + vmem(1),
        vmem(1),
        [
            pltpu.SMEM((SLABS, 128), jnp.int32),
            pltpu.VMEM((count, RHS // 2, 128), bf16),
            pltpu.VMEM((SLABS, RANK, 128), bf16),
            dma((3,)),
        ],
    )(pin(owner, HBM), pin(tops, HBM), pin(matrix, HBM), transfer)
    (out,) = call(
        far_kernel,
        "far",
        [((LEAVES, RHS, PART), f32)],
        vmem(4),
        vmem(1),
        [],
    )(pin(parts, pltpu.VMEM), extra, jnp.swapaxes(basis_out, 1, 2), near)
    return out


COLUMNS = 8


def solution(mesh):
    grid = mesh.devices.reshape(-1, COLUMNS, mesh.shape["slab"])
    morton = ("z", "y")
    return jax.shard_map(
        shards,
        mesh=Mesh(grid, ("z", "y", "slab")),
        in_specs=(
            P(morton, None, "slab"),
            P(morton, None, "slab"),
            P(morton, None, "slab"),
            P(morton, None, None),
            P(morton, "slab", None, None),
            P(morton, "slab"),
            P(morton, "slab", None),
            P(morton),
            P(morton),
            P(morton),
            P(morton),
        ),
        out_specs=P(morton, None, "slab"),
        check_vma=False,
    )
```

```python
import jax
import jax.numpy as jnp
from jax import lax
from jax.experimental import pallas as pl
from jax.experimental.pallas import tpu as pltpu
from jax.sharding import Mesh, PartitionSpec as P

LEAVES = 16
CLUSTERS = 31
RANK = 64
RHS = 32
POINTS = 256
SLABS = 8
PART = POINTS // SLABS
PAIRS = 15
HALF = 15
LEVELS = ((0, 8), (16, 4), (24, 2), (28, 1))
SRC_ROWS = LEAVES * RHS * PART // 128
BASIS_ROWS = LEAVES * PART * RANK // 128
TOP_ROW = SRC_ROWS + BASIS_ROWS
OWNER_ROW = TOP_ROW + RANK
PACKED = OWNER_ROW + 16
TILE_SLOTS = 48
NEAR_CHUNKS = 4
bf16 = jnp.bfloat16
f32 = jnp.float32
MIB = 1024 * 1024
pin = pltpu.with_memory_space_constraint
HBM = pltpu.HBM
NT = (((1,), (1,)), ((), ()))
NN = (((1,), (0,)), ((), ()))


def dot(a, b, dims):
    return lax.dot_general(a, b, dims, preferred_element_type=f32)


def split(x):
    high = x.astype(bf16)
    return high, (x - high.astype(f32)).astype(bf16)


def dot3(a, b, dims):
    a_high, a_low = a
    b_high, b_low = b
    rows = a_high.shape[0]
    both = dot(jnp.concatenate([a_high, a_low], axis=0), b_high, dims)
    return both[:rows] + both[rows:] + dot(a_high, b_low, dims)


def pair_matrices(transfer_ref, i):
    return jnp.concatenate([transfer_ref[2 * i], transfer_ref[2 * i + 1]], axis=1)


def climb(pairs, transfer_ref, keep):
    first = 0
    count = LEAVES // 2
    while True:
        parents = []
        for i in range(first, first + count):
            parts = split(pairs[i])
            keep(i, parts)
            parents.append(dot3(parts, split(pair_matrices(transfer_ref, i)), NT))
        if count == 1:
            return parents[0]
        first = first + count
        count = count // 2
        for i in range(count):
            pairs.append(jnp.concatenate([parents[2 * i], parents[2 * i + 1]], axis=1))


def descend(level, transfer_ref):
    first = PAIRS - 1
    while first > 0:
        parents = []
        for pair in level:
            parents.append(pair[:, :RANK])
            parents.append(pair[:, RANK:])
        first = first - len(parents)
        level = []
        for i, parent in enumerate(parents):
            passed = dot3(split(parent), split(pair_matrices(transfer_ref, first + i)), NN)
            level.append(passed)
    return level


def leaf_pair(sources, basis):
    product = dot(jnp.concatenate(sources, axis=0), basis, NN)
    left = lax.broadcasted_iota(jnp.int32, (RHS, 128), 1) < RANK
    return jnp.where(left, product[:RHS], product[RHS:])


def fetch(pairs, sems):
    copies = [
        pltpu.make_async_copy(src, dst, sems.at[k]) for k, (src, dst) in enumerate(pairs)
    ]
    for copy in copies:
        copy.start()
    return copies


def pack_kernel(
    list_hbm,
    sources_hbm,
    basis_hbm,
    coupling_hbm,
    out_hbm,
    out_ref,
    sources_ref,
    basis_ref,
    coupling_ref,
    list_ref,
    in_sem,
    out_sem,
):
    copies = fetch(
        (
            (sources_hbm, sources_ref),
            (basis_hbm, basis_ref),
            (coupling_hbm.at[CLUSTERS - 1], coupling_ref),
            (list_hbm, list_ref),
        ),
        in_sem,
    )
    for copy in copies:
        copy.wait()
    for g in range(LEAVES // 4):
        out_ref[g * RHS : (g + 1) * RHS, :] = jnp.concatenate(
            [sources_ref[4 * g + i] for i in range(4)], axis=1
        )
    for i in range(LEAVES // 2):
        start = SRC_ROWS + i * PART
        out_ref[start : start + PART, :] = jnp.concatenate(
            [basis_ref[2 * i], basis_ref[2 * i + 1]], axis=1
        )
    out_ref[TOP_ROW : TOP_ROW + RANK, :] = jnp.concatenate(
        [coupling_ref[0], coupling_ref[1]], axis=1
    ).astype(bf16)
    row = lax.broadcasted_iota(jnp.int32, (16, 128), 0)
    lane = lax.broadcasted_iota(jnp.int32, (16, 128), 1)
    first_cluster = morton_index() * CLUSTERS - CLUSTERS
    listed = jnp.zeros((16, 128), jnp.int32)
    for e in range(2):
        owner = lax.shift_right_logical(list_ref[e, CLUSTERS - 1] * 2115, 16)
        listed = jnp.where((row == 0) & (lane == e), owner, listed)
        here = row == 1 + e
        for g in range(CLUSTERS - 1):
            listed = jnp.where(here & (lane == g), list_ref[e, g] - first_cluster, listed)
    out_ref[OWNER_ROW : OWNER_ROW + 16, :] = listed.astype(f32).astype(bf16)
    out = pltpu.make_async_copy(out_ref, out_hbm, out_sem.at[0])
    out.start()
    out.wait()


def share_kernel(coupling_hbm, received_hbm, share_hbm, share_ref, half_ref, half_sem, out_sem):
    del received_hbm
    halves = fetch(
        [
            (coupling_hbm.at[pl.ds(source, count)], half_ref.at[pl.ds(place, count)])
            for place, source, count in half_of(1 - lax.axis_index("slab") % 2)
        ],
        half_sem,
    )
    for copy in halves:
        copy.wait()
    for i in range(HALF):
        share_ref[i] = jnp.concatenate([half_ref[i, 0], half_ref[i, 1]], axis=1)
    share = pltpu.make_async_copy(share_ref, share_hbm, out_sem)
    share.start()
    share.wait()


def up_kernel(
    packed_ref,
    transfer_ref,
    mine_hbm,
    top_hbm,
    matrix_hbm,
    owner_ref,
    mine_ref,
    top_ref,
    out_sem,
):
    out_matrix = pltpu.make_async_copy(
        packed_ref.at[:, pl.ds(TOP_ROW, RANK)], matrix_hbm, out_sem.at[3]
    )
    out_matrix.start()
    for g in range(LEAVES // 4):
        tiles = [packed_ref[s, g * RHS : (g + 1) * RHS, :] for s in range(SLABS)]
        for i in range(4):
            mine_ref[4 * g + i] = jnp.concatenate(
                [t[:, i * PART : (i + 1) * PART] for t in tiles], axis=1
            )
    rows = pl.ds(0, LEAVES)
    out_rows = pltpu.make_async_copy(mine_ref.at[rows], mine_hbm.at[rows], out_sem.at[0])
    out_rows.start()
    pairs = []
    for i in range(LEAVES // 2):
        start = SRC_ROWS + i * PART
        basis = jnp.concatenate(
            [packed_ref[s, start : start + PART, :] for s in range(SLABS)], axis=0
        )
        pairs.append(leaf_pair([mine_ref[2 * i], mine_ref[2 * i + 1]], basis))

    def keep(i, parts):
        mine_ref[LEAVES + i] = jnp.concatenate(parts, axis=1)

    top = climb(pairs, transfer_ref, keep).astype(bf16)
    rows = pl.ds(LEAVES, PAIRS)
    out_pairs = pltpu.make_async_copy(mine_ref.at[rows], mine_hbm.at[rows], out_sem.at[1])
    out_pairs.start()
    row = jnp.concatenate([top[: RHS // 2], top[RHS // 2 :]], axis=1)
    top_ref[...] = jnp.broadcast_to(row[None], top_ref.shape)
    out_top = pltpu.make_async_copy(top_ref, top_hbm, out_sem.at[2])
    out_top.start()
    for s in range(SLABS):
        owner_ref[s : s + 1, :] = packed_ref[s, OWNER_ROW:].astype(f32)[:1].astype(jnp.int32)
    other = packed_ref[lax.axis_index("slab") ^ 1, OWNER_ROW:].astype(f32)
    owner_ref[SLABS : 2 * SLABS, :] = other[:SLABS].astype(jnp.int32)
    out_rows.wait()
    out_pairs.wait()
    out_top.wait()
    out_matrix.wait()


def half_of(half):
    place = 0
    runs = []
    for first, count in LEVELS:
        runs.append((place, first + half * count, count))
        place += count
    return runs


def field_kernel(
    list_hbm,
    other_hbm,
    mine_hbm,
    received_hbm,
    swapped_hbm,
    scale_hbm,
    target_hbm,
    source_hbm,
    count_hbm,
    near_hbm,
    share_ref,
    transfer_ref,
    coupling_ref,
    leaf_hbm,
    out_ref,
    list_ref,
    other_ref,
    window_ref,
    high_ref,
    low_ref,
    leaf_ref,
    scale_ref,
    target_ref,
    source_ref,
    count_ref,
    rows_ref,
    near_ref,
    in_sem,
    near_sem,
    out_sem,
):
    copies = fetch(
        [
            (hbm.at[pl.ds(LEAVES, PAIRS)], window_ref.at[pl.ds(k * PAIRS, PAIRS)])
            for k, hbm in zip(window_places(), (mine_hbm, received_hbm, swapped_hbm))
        ]
        + [
            (list_hbm, list_ref),
            (other_hbm.at[pl.ds(SLABS, SLABS)], other_ref),
        ],
        in_sem,
    )
    chunk = near_ref.shape[0] // NEAR_CHUNKS
    near_copies = fetch(
        [
            (scale_hbm, scale_ref),
            (target_hbm, target_ref),
            (source_hbm, source_ref),
            (count_hbm, count_ref),
        ]
        + [
            (hbm.at[pl.ds(0, LEAVES)], rows_ref.at[pl.ds(k * LEAVES, LEAVES)])
            for k, hbm in zip(window_places(), (mine_hbm, received_hbm, swapped_hbm))
        ]
        + [
            (near_hbm.at[pl.ds(k * chunk, chunk)], near_ref.at[pl.ds(k * chunk, chunk)])
            for k in range(NEAR_CHUNKS)
        ],
        near_sem,
    )
    out_ref[...] = jnp.zeros_like(out_ref)
    runs = half_of(lax.axis_index("slab") % 2)
    for start, first, count in runs:
        for i in range(count):
            matrices = jnp.concatenate(
                [coupling_ref[first + i, 0], coupling_ref[first + i, 1], share_ref[start + i]],
                axis=1,
            )
            high_ref[start + i], low_ref[start + i] = split(matrices)
    left = lax.broadcasted_iota(jnp.int32, (RHS, 128), 1) < RANK
    first_cluster = morton_index() * CLUSTERS - CLUSTERS
    for copy in copies:
        copy.wait()

    def swapped(x):
        return jnp.concatenate([x[:, RANK:], x[:, :RANK]], axis=1)

    def pick(local, e):
        owner = (local >= CLUSTERS).astype(jnp.int32) + (local >= 2 * CLUSTERS).astype(
            jnp.int32
        )
        cluster = local - owner * CLUSTERS
        pair = lax.shift_right_logical(cluster, 1)
        block = window_ref[owner * PAIRS + pair]
        high, low = block[:, :128], block[:, 128:]
        here = (cluster - 2 * pair) == e
        return jnp.where(here, high, swapped(high)), jnp.where(here, low, swapped(low))

    def pick_two(locals_of):
        (high0, low0), (high1, low1) = pick(locals_of(0), 0), pick(locals_of(1), 1)
        return jnp.where(left, high0, high1), jnp.where(left, low0, low1)

    def coupled(place, g):
        own = pick_two(lambda e: list_ref[e, g] - first_cluster)
        other = pick_two(lambda e: other_ref[1 + e, g])
        picked = [jnp.concatenate([x, y], axis=1) for x, y in zip(own, other)]
        return dot3(picked, (high_ref[place], low_ref[place]), NT)

    place, g, _ = runs[-1]
    level = [coupled(place, g)]
    for place, first, count in reversed(runs[:-1]):
        parents, level = level, []
        for i, parent in enumerate(parents):
            own = [coupled(place + 2 * i + k, first + 2 * i + k) for k in range(2)]
            pair = lax.shift_right_logical(first, 1) + i
            passed = dot3(split(parent), split(pair_matrices(transfer_ref, pair)), NN)
            total = jnp.concatenate(own, axis=1) + passed
            level += [total] if count == LEAVES // 2 else [total[:, :RANK], total[:, RANK:]]
    for i in range(LEAVES // 4):
        leaf_ref[i * RHS : (i + 1) * RHS, :] = level[i].astype(bf16)
    leaf_copies = fetch([(leaf_ref, leaf_hbm.at[s]) for s in range(SLABS)], out_sem)

    morton = morton_index()
    first_source = (morton - 1) * LEAVES
    first_target = morton * LEAVES
    for copy in near_copies[:-NEAR_CHUNKS]:
        copy.wait()
    live = count_ref[0]

    def tile(t, carry):
        base = t * TILE_SLOTS
        products = []
        for k in range(TILE_SLOTS):
            slot = base + k
            row = source_ref[slot] - first_source
            products.append(dot(rows_ref[row], near_ref[slot], NT))
        for k in range(TILE_SLOTS):
            slot = base + k
            target = target_ref[slot] - first_target
            weight = jnp.where(slot < live, scale_ref[slot], 0.0)
            out_ref[target] += weight * products[k]
        return carry

    tiles = (live + TILE_SLOTS - 1) // TILE_SLOTS
    step = chunk // TILE_SLOTS
    for k in range(NEAR_CHUNKS):
        near_copies[k - NEAR_CHUNKS].wait()
        lax.fori_loop(k * step, jnp.clip(tiles, k * step, (k + 1) * step), tile, 0)
    for copy in leaf_copies:
        copy.wait()


def top_kernel(
    owner_hbm,
    tops_hbm,
    matrix_hbm,
    transfer_ref,
    extra_ref,
    owner_ref,
    tops_ref,
    matrix_ref,
    in_sem,
):
    copies = fetch(
        (
            (owner_hbm.at[pl.ds(0, SLABS)], owner_ref),
            (tops_hbm, tops_ref),
            (matrix_hbm, matrix_ref),
        ),
        in_sem,
    )
    for copy in copies:
        copy.wait()

    def top_of(s, e):
        block = tops_ref[owner_ref[s, e]]
        return jnp.concatenate([block[:, :RANK], block[:, RANK:]], axis=0)

    top = jnp.zeros((RHS, RANK), f32)
    for s in range(SLABS):
        picked = jnp.concatenate([top_of(s, 0), top_of(s, 1)], axis=1)
        top = top + dot(picked, matrix_ref[s], NT)
    matrices = split(pair_matrices(transfer_ref, PAIRS - 1))
    level = descend([dot3(split(top), matrices, NN)], transfer_ref)
    for i in range(LEAVES // 2):
        extra_ref[i] = level[i]


def far_kernel(parts_ref, extra_ref, basis_ref, near_ref, out_ref):
    for i in range(LEAVES // 2):
        half, place = divmod(i, LEAVES // 4)
        rows = pl.ds(place * RHS, RHS)
        total = extra_ref[i]
        for s in range(half, SLABS, 2):
            total = total + parts_ref[s, rows, :].astype(f32)
        high, low = split(total)
        both = jnp.concatenate([high, low], axis=0)
        for k in range(2):
            leaf = 2 * i + k
            product = dot(both[:, k * RANK : (k + 1) * RANK], basis_ref[leaf], NT)
            out_ref[leaf] = near_ref[leaf] + (product[:RHS] + product[RHS:])


def window_places():
    odd = lax.axis_index("slab") % 2
    return 1, 2 * odd, 2 - 2 * odd


def morton_index():
    return lax.axis_index(("z", "y"))


def vmem(n):
    return [pl.BlockSpec(memory_space=pltpu.VMEM)] * n


def smem(n):
    return [pl.BlockSpec(memory_space=pltpu.SMEM)] * n


def hbm(n):
    return [pl.BlockSpec(memory_space=pltpu.HBM)] * n


def shards(
    sources,
    basis_in,
    basis_out,
    transfer,
    coupling,
    coupling_list,
    near_block,
    near_scale,
    near_target,
    near_source,
    near_count,
):
    height, columns = lax.axis_size("z"), lax.axis_size("y")
    count = height * columns
    slots = near_block.shape[0]
    listed = coupling_list.T
    dma = pltpu.SemaphoreType.DMA

    def call(kernel, name, outs, in_specs, out_specs, scratch, limit=40, **params):
        return pl.pallas_call(
            kernel,
            out_shape=tuple(
                out[2](*out[:2]) if out[2:] else jax.ShapeDtypeStruct(*out)
                for out in outs
            ),
            in_specs=in_specs,
            out_specs=tuple(out_specs),
            scratch_shapes=scratch,
            compiler_params=pltpu.CompilerParams(vmem_limit_bytes=limit * MIB),
            name=name,
            **params,
        )

    (packed,) = call(
        pack_kernel,
        "pack",
        [((PACKED, 128), bf16, HBM)],
        hbm(4),
        hbm(1),
        [
            pltpu.VMEM((PACKED, 128), bf16),
            pltpu.VMEM(sources.shape, bf16),
            pltpu.VMEM((LEAVES, PART, RANK), bf16),
            pltpu.VMEM(coupling.shape[1:], f32),
            pltpu.SMEM(listed.shape, jnp.int32),
            dma((4,)),
            dma((1,)),
        ],
    )(
        pin(listed, HBM),
        pin(sources, HBM),
        pin(jnp.swapaxes(basis_in, 1, 2), HBM),
        pin(coupling, HBM),
    )
    gathered = lax.all_gather(packed, "slab")
    mine, top, matrix, owner = call(
        up_kernel,
        "up",
        [
            ((LEAVES + PAIRS, RHS, POINTS), bf16, HBM),
            ((count, RHS // 2, 128), bf16, HBM),
            ((SLABS, RANK, 128), bf16, HBM),
            ((2 * SLABS, 128), jnp.int32),
        ],
        vmem(2),
        hbm(3) + vmem(1),
        [
            pltpu.VMEM((LEAVES + PAIRS, RHS, POINTS), bf16),
            pltpu.VMEM((count, RHS // 2, 128), bf16),
            dma((4,)),
        ],
    )(pin(gathered, pltpu.VMEM), transfer)
    moves = []
    for m in range(count):
        for s in range(SLABS):
            to = m + 1 - 2 * (s % 2)
            if 0 <= to < count:
                moves.append((m * SLABS + s, to * SLABS + s))
    received = lax.ppermute(mine, ("z", "y", "slab"), moves)
    swapped = lax.ppermute(received, "slab", [(s, s ^ 1) for s in range(SLABS)])
    (share,) = call(
        share_kernel,
        "share",
        [((HALF, RANK, 128), f32, HBM)],
        hbm(2),
        hbm(1),
        [
            pltpu.VMEM((HALF, RANK, 128), f32),
            pltpu.VMEM((HALF, *coupling.shape[1:]), f32),
            dma((len(LEVELS),)),
            dma,
        ],
    )(pin(coupling, HBM), pin(received, HBM))
    share = lax.ppermute(share, "slab", [(s, s ^ 1) for s in range(SLABS)])
    mine, received, swapped = pin(mine, HBM), pin(received, HBM), pin(swapped, pltpu.VMEM)
    tops = lax.all_to_all(top, ("z", "y"), 0, 0)
    leaf, near = call(
        field_kernel,
        "field",
        [((SLABS, LEAVES // 4 * RHS, 128), bf16, HBM), ((LEAVES, RHS, PART), f32)],
        hbm(10) + vmem(3),
        hbm(1) + vmem(1),
        [
            pltpu.SMEM(listed.shape, jnp.int32),
            pltpu.SMEM((SLABS, 128), jnp.int32),
            pltpu.VMEM((3 * PAIRS, RHS, 256), bf16),
            pltpu.VMEM((HALF, RANK, 256), bf16),
            pltpu.VMEM((HALF, RANK, 256), bf16),
            pltpu.VMEM((LEAVES // 4 * RHS, 128), bf16),
            pltpu.SMEM((slots,), f32),
            pltpu.SMEM((slots,), jnp.int32),
            pltpu.SMEM((slots,), jnp.int32),
            pltpu.SMEM((1,), jnp.int32),
            pltpu.VMEM((3 * LEAVES, RHS, POINTS), bf16),
            pltpu.VMEM((slots, PART, POINTS), bf16),
            dma((5,)),
            dma((7 + NEAR_CHUNKS,)),
            dma((SLABS,)),
        ],
    )(
        listed,
        owner,
        mine,
        received,
        swapped,
        pin(near_scale, HBM),
        pin(near_target, HBM),
        pin(near_source, HBM),
        near_count,
        pin(near_block, HBM),
        pin(share, pltpu.VMEM),
        transfer,
        coupling,
    )
    parts = lax.all_to_all(leaf, "slab", 0, 0)
    (extra,) = call(
        top_kernel,
        "top",
        [((LEAVES // 2, RHS, 128), f32)],
        hbm(3) + vmem(1),
        vmem(1),
        [
            pltpu.SMEM((SLABS, 128), jnp.int32),
            pltpu.VMEM((count, RHS // 2, 128), bf16),
            pltpu.VMEM((SLABS, RANK, 128), bf16),
            dma((3,)),
        ],
    )(pin(owner, HBM), pin(tops, HBM), pin(matrix, HBM), transfer)
    (out,) = call(
        far_kernel,
        "far",
        [((LEAVES, RHS, PART), f32)],
        vmem(4),
        vmem(1),
        [],
    )(pin(parts, pltpu.VMEM), extra, jnp.swapaxes(basis_out, 1, 2), near)
    return out


COLUMNS = 8


def solution(mesh):
    grid = mesh.devices.reshape(-1, COLUMNS, mesh.shape["slab"])
    morton = ("z", "y")
    return jax.shard_map(
        shards,
        mesh=Mesh(grid, ("z", "y", "slab")),
        in_specs=(
            P(morton, None, "slab"),
            P(morton, None, "slab"),
            P(morton, None, "slab"),
            P(morton, None, None),
            P(morton, "slab", None, None),
            P(morton, "slab"),
            P(morton, "slab", None),
            P(morton),
            P(morton),
            P(morton),
            P(morton),
        ),
        out_specs=P(morton, None, "slab"),
        check_vma=False,
    )
```
